32 devices in a mesh: groups: 2 (over y), head: 4 (over x, core), dp: 4 (over z).
Axes of the slice: x: 2, y: 2, z: 4, core: 2. Of those that a mesh axis runs over, the one named last changes fastest.
Arguments:
- queries: bfloat16 [8, 512, 12288], P(('groups', 'dp'), None, 'head'), parts along dimension 0, may hold values from -8 to 8
- out_grad: bfloat16 [8, 512, 8192], P(('groups', 'dp'), None, 'head'), parts along dimension 0, may hold values from -6 to 6
- latent: bfloat16 [8, 512, 576], P(('groups', 'dp'), 'head'), parts along dimension 0, may hold values from -8 to 8
- w_uk: bfloat16 [512, 8192], P(None, 'head'), may hold values from -0.25 to 0.25
- w_uv: bfloat16 [512, 8192], P(None, 'head'), may hold values from -0.25 to 0.25
- lengths: int32 [8], P(('groups', 'dp')), parts along dimension 0, may hold values from 128 to 512
- rewards: float32 [8], P('groups'), parts along dimension 0, may hold values from -6 to 6
- pairing: int32 [8], P('groups'), parts along dimension 0, may hold values from 0 to 3, each once
Outputs:
- q_grad: bfloat16 [8, 512, 12288], P(('groups', 'dp'), None, 'head'), parts along dimension 0
- latent_grad: bfloat16 [8, 512, 576], P(('groups', 'dp'), 'head'), parts along dimension 0
- uk_grad: float32 [1024, 8192], P(('groups', 'dp'), 'head'), parts along dimension 0
- uv_grad: float32 [1024, 8192], P(('groups', 'dp'), 'head'), parts along dimension 0
The draws below stay inside these ranges and needn't reach their ends.
There are 2 independent parts, one for each index of `groups`. The reference program is written for one: setup_inputs(seed, part) draws one part's arguments, and reference() takes and returns one part's arrays. A program takes and returns all parts, laid end to end along the dimension named above; an argument that names none is the same for every part. Nothing has to cross between parts.
All inputs are finite; a program needn't handle non-finite values.
Results may differ from the reference program's by a relative error of at most 0.008.
Values may be sent and summed in bfloat16 or wider, within the bound.
A program may use at most 64 MiB of HBM per device.

```python
import jax
import jax.numpy as jnp
from jax import lax

L = 512
HEADS = 64
D_C = 512
D_R = 64
DN = 128
DV = 128
SEQS = 4


def draw_latent(key, part):
    shape = (SEQS, L, D_C + D_R)
    base = jnp.clip(jax.random.normal(jax.random.fold_in(key, 1), shape, jnp.float32), -6.0, 6.0)
    return base.astype(jnp.bfloat16)


def draw_queries(key, part):
    shape = (SEQS, L, HEADS, DN + D_R)
    base = jnp.clip(jax.random.normal(jax.random.fold_in(key, 2), shape, jnp.float32), -6.0, 6.0)
    return base.reshape(SEQS, L, HEADS * (DN + D_R)).astype(jnp.bfloat16)


def touch_ends(values, stream_key, smallest, high):
    place = [jax.random.randint(jax.random.fold_in(stream_key, axis), (), 0, length) for axis, length in enumerate(values.shape)]
    longest = values.shape.index(max(values.shape))
    neighbour = place[:longest] + [(place[longest] + 1) % values.shape[longest]] + place[longest + 1:]
    return values.at[tuple(place)].set(smallest).at[tuple(neighbour)].set(high)


def block_levels(own_key, extent, pieces, low, top_value):
    def one(axis_at, blocks):
        heights = jax.random.uniform(jax.random.fold_in(jax.random.fold_in(own_key, 6), axis_at), (blocks,), jnp.float32, low / len(pieces), top_value / len(pieces))
        return jnp.repeat(jnp.exp(heights), extent[axis_at] // blocks).reshape((-1,) + (1,) * (len(extent) - axis_at - 1))

    gain = one(*pieces[0])
    for cut in pieces[1:]:
        gain = gain * one(*cut)
    return gain


def centred(key, dims, scale, reach, split=(), held_as=jnp.bfloat16):
    drawn = scale * jax.random.normal(key, dims, jnp.float32)
    if split:
        drawn = drawn * block_levels(key, dims, split, -0.22, 0.18)
    return jnp.clip(drawn, -reach, reach).astype(held_as)


def setup_inputs(seed: int = 0, part: int = 0) -> dict:
    seeds = jax.random.split(jax.random.key(seed), 9)
    part_splits = jax.random.split(jax.random.fold_in(seeds[8], part), 9)
    return {
        "queries": draw_queries(jax.random.fold_in(jax.random.fold_in(seeds[8], part), 71), part),
        "out_grad": centred(part_splits[1], (SEQS, L, HEADS * DV), 1.0, 6.0, ((0, 4), (2, 4))),
        "latent": draw_latent(jax.random.fold_in(jax.random.fold_in(seeds[8], part), 71), part),
        "w_uk": centred(seeds[3], (D_C, HEADS * DN), D_C ** -0.5, 0.25, ((1, 4),)),
        "w_uv": centred(seeds[4], (D_C, HEADS * DV), D_C ** -0.5, 0.25, ((1, 4),)),
        "lengths": touch_ends(jax.random.randint(part_splits[5], (SEQS,), L // 4, L + 1), jax.random.fold_in(part_splits[5], 1), L // 4, L).astype(jnp.int32),
        "rewards": centred(part_splits[6], (SEQS,), 2.0, 6.0, (), jnp.float32),
        "pairing": jax.random.permutation(part_splits[7], SEQS).astype(jnp.int32),
    }


def pair_weights(rewards, pairing):
    count = pairing.shape[0]
    onehot = (pairing[:, None] == jnp.arange(count, dtype=jnp.int32)[None, :]).astype(jnp.float32)
    ordered = jnp.sum(onehot * rewards[None, :], axis=1)
    push = jax.nn.sigmoid(ordered[1::2] - ordered[0::2])
    in_order = jnp.stack([-push, push], axis=1).reshape(count)
    return jnp.sum(onehot * in_order[:, None], axis=0)


def head_backward(query_head, grad_head, key_head, value_head, rope_keys, valid):
    factor = (DN + D_R) ** -0.5
    scores = jnp.dot(query_head[:, :DN], key_head.T, preferred_element_type=jnp.float32)
    scores = scores + jnp.dot(query_head[:, DN:], rope_keys.T, preferred_element_type=jnp.float32)
    scores = jnp.where(valid, scores * factor, -1e30)
    top = jnp.max(scores, axis=1, keepdims=True)
    expo = jnp.exp(scores - top)
    prob = expo / jnp.sum(expo, axis=1, keepdims=True)
    prob_b = prob.astype(jnp.bfloat16)
    dprob = jnp.dot(grad_head, value_head.T, preferred_element_type=jnp.float32)
    delta = jnp.sum(prob * dprob, axis=1, keepdims=True)
    dscore = (prob * (dprob - delta)).astype(jnp.bfloat16)
    dq_nope = jnp.dot(dscore, key_head, preferred_element_type=jnp.float32)
    dq_rope = jnp.dot(dscore, rope_keys, preferred_element_type=jnp.float32)
    dquery = (jnp.concatenate([dq_nope, dq_rope], axis=1) * factor).astype(jnp.bfloat16)
    dkey = (jnp.dot(dscore.T, query_head[:, :DN], preferred_element_type=jnp.float32) * factor).astype(jnp.bfloat16)
    drope = jnp.dot(dscore.T, query_head[:, DN:], preferred_element_type=jnp.float32) * factor
    dvalue = jnp.dot(prob_b.T, grad_head, preferred_element_type=jnp.float32).astype(jnp.bfloat16)
    return dquery, dkey, dvalue, drope


def sequence_attention(query_rows, grad_rows, keys, values, rope_keys, length, weight, heads):
    where = jnp.arange(L, dtype=jnp.int32)
    valid = (where[None, :] <= where[:, None]) & (where[None, :] < length)
    rowmask = (where < length).astype(jnp.float32)
    scaled = (grad_rows.astype(jnp.float32) * weight * rowmask[:, None]).astype(jnp.bfloat16)
    query_heads = query_rows.reshape(L, heads, DN + D_R).transpose(1, 0, 2)
    grad_heads = scaled.reshape(L, heads, DV).transpose(1, 0, 2)
    key_heads = keys.reshape(L, heads, DN).transpose(1, 0, 2)
    value_heads = values.reshape(L, heads, DV).transpose(1, 0, 2)

    def one_head(items):
        return head_backward(items[0], items[1], items[2], items[3], rope_keys, valid)

    dquery, dkey, dvalue, drope = lax.map(one_head, (query_heads, grad_heads, key_heads, value_heads))
    dquery = dquery.transpose(1, 0, 2).reshape(L, heads * (DN + D_R))
    dkey = dkey.transpose(1, 0, 2).reshape(L, heads * DN)
    dvalue = dvalue.transpose(1, 0, 2).reshape(L, heads * DV)
    return dquery, dkey, dvalue, jnp.sum(drope, axis=0)


def reference(queries, out_grad, latent, w_uk, w_uv, lengths, rewards, pairing):
    weights = pair_weights(rewards, pairing)

    def step(carry, items):
        query_rows, grad_rows, latent_rows, length, weight = items
        content = latent_rows[:, :D_C]
        rope_keys = latent_rows[:, D_C:]
        keys = jnp.dot(content, w_uk, preferred_element_type=jnp.float32).astype(jnp.bfloat16)
        values = jnp.dot(content, w_uv, preferred_element_type=jnp.float32).astype(jnp.bfloat16)
        dquery, dkey, dvalue, drope = sequence_attention(query_rows, grad_rows, keys, values, rope_keys, length, weight, HEADS)
        dcontent = jnp.dot(dkey, w_uk.T, preferred_element_type=jnp.float32)
        dcontent = dcontent + jnp.dot(dvalue, w_uv.T, preferred_element_type=jnp.float32)
        lat_grad = jnp.concatenate([dcontent, drope], axis=1).astype(jnp.bfloat16)
        uk_sum = carry[0] + jnp.dot(content.T, dkey, preferred_element_type=jnp.float32)
        uv_sum = carry[1] + jnp.dot(content.T, dvalue, preferred_element_type=jnp.float32)
        return (uk_sum, uv_sum), (dquery, lat_grad)

    start = (jnp.zeros((D_C, HEADS * DN), jnp.float32), jnp.zeros((D_C, HEADS * DV), jnp.float32))
    sums, outs = lax.scan(step, start, (queries, out_grad, latent, lengths, weights))
    return outs[0], outs[1], sums[0], sums[1]
```

```python
import functools

import jax
import jax.numpy as jnp
from jax import lax
from jax.experimental import pallas as pl
from jax.experimental.pallas import tpu as pltpu
from jax.sharding import PartitionSpec as P

D_C = 512
D_R = 64
DN = 128
DV = 128
BLK = 256
MESH = pl.DeviceIdType.MESH
F32 = jnp.float32
BF16 = jnp.bfloat16


def dot_nn(a, b):
    return lax.dot_general(a, b, (((1,), (0,)), ((), ())), preferred_element_type=F32)


def dot_nt(a, b):
    return lax.dot_general(a, b, (((1,), (1,)), ((), ())), preferred_element_type=F32)


def dot_tn(a, b):
    return lax.dot_general(a, b, (((0,), (0,)), ((), ())), preferred_element_type=F32)


def own_weight(rewards, pairing, own):
    count = rewards.shape[0]
    diff = jnp.float32(0.0)
    sign = jnp.float32(0.0)
    for k in range(count // 2):
        chosen, rejected = pairing[2 * k], pairing[2 * k + 1]
        gap = jnp.float32(0.0)
        for j in range(count):
            gap = gap + jnp.where(rejected == j, rewards[j], 0.0)
            gap = gap - jnp.where(chosen == j, rewards[j], 0.0)
        diff = jnp.where((chosen == own) | (rejected == own), gap, diff)
        sign = jnp.where(chosen == own, -1.0, jnp.where(rejected == own, 1.0, sign))
    return sign * jax.nn.sigmoid(jnp.full((1, DV), diff, F32))


def kernel(
    n_head, n_dp, pairs,
    lengths, rewards, pairing, latent, q, og, wk, wv,
    qg, lg, uk, uv,
    full, cont_t, send, recv, dkv, rope_acc, lacc, lrecv,
    g_send, g_recv, p_send, p_recv, l_send, l_recv,
):
    factor = (DN + D_R) ** (-0.5)
    me_h = lax.axis_index("head")
    me_d = lax.axis_index("dp")
    tokens = latent.shape[0]
    length_all = full.shape[0]
    blocks = length_all // BLK

    barrier = pltpu.get_barrier_semaphore()
    for o in range(1, n_head):
        pl.semaphore_signal(
            barrier, inc=1, device_id={"head": lax.rem(me_h + o, n_head)}, device_id_type=MESH
        )
    for o in range(1, n_dp):
        pl.semaphore_signal(
            barrier, inc=1, device_id={"dp": lax.rem(me_d + o, n_dp)}, device_id_type=MESH
        )
    pl.semaphore_wait(barrier, n_head + n_dp - 2)

    own_rows = pl.ds(pl.multiple_of(me_h * tokens, tokens), tokens)

    def gather(o):
        return pltpu.make_async_remote_copy(
            src_ref=latent,
            dst_ref=full.at[own_rows],
            send_sem=g_send.at[o - 1],
            recv_sem=g_recv.at[o - 1],
            device_id={"head": lax.rem(me_h + o, n_head)},
            device_id_type=MESH,
        )

    def partial(p, o):
        peer = lax.rem(me_d + o, n_dp)
        return pltpu.make_async_remote_copy(
            src_ref=send.at[p, peer],
            dst_ref=recv.at[p, o - 1],
            send_sem=p_send.at[p, o - 1],
            recv_sem=p_recv.at[p, o - 1],
            device_id={"dp": peer},
            device_id_type=MESH,
        )

    def latent_part(o):
        peer = lax.rem(me_h + o, n_head)
        return pltpu.make_async_remote_copy(
            src_ref=lacc.at[peer],
            dst_ref=lrecv.at[o - 1],
            send_sem=l_send.at[o - 1],
            recv_sem=l_recv.at[o - 1],
            device_id={"head": peer},
            device_id_type=MESH,
        )

    for o in range(1, n_head):
        gather(o).start()
    full[own_rows, :] = latent[...]
    length = lengths[0]
    weight = own_weight(rewards, pairing, me_d)
    rope_acc[...] = jnp.zeros_like(rope_acc)
    for o in range(1, n_head):
        gather(o).wait()
    cont_t[...] = full[:, :D_C].T

    def body(p, carry):
        cols = pl.ds(pl.multiple_of(p * 2 * DN, 2 * DN), 2 * DN)
        qcols = pl.ds(pl.multiple_of(p * 2 * (DN + D_R), 2 * (DN + D_R)), 2 * (DN + D_R))
        content = full[:, :D_C]
        rope = full[:, D_C:]
        k2 = dot_nn(content, wk[:, cols]).astype(BF16)
        v2 = dot_nn(content, wv[:, cols]).astype(BF16)
        empty = jnp.zeros((length_all, D_R), BF16)
        keys = (
            jnp.concatenate([k2[:, :DN], rope, empty], axis=1),
            jnp.concatenate([empty, k2[:, DN:], rope], axis=1),
        )
        row = lax.broadcasted_iota(jnp.int32, (length_all, 2 * DV), 0)
        w2 = jnp.concatenate([weight, weight], axis=1)
        g2 = og[:, cols].astype(F32) * w2
        g2 = jnp.where(row < length, g2, 0.0).astype(BF16)
        dks, dvs = [], []
        dqs = [[], []]
        for side in range(2):
            kx = keys[side]
            vx = v2[:, side * DV : (side + 1) * DV]
            dk = [None] * blocks
            dv = [None] * blocks
            for b in range(blocks):
                reach = (b + 1) * BLK
                rows = slice(b * BLK, reach)
                qx = q[rows, qcols][:, side * DN : side * DN + 2 * DN]
                gx = g2[rows, side * DV : (side + 1) * DV]
                at_j = lax.broadcasted_iota(jnp.int32, (reach, BLK), 0)
                at_i = lax.broadcasted_iota(jnp.int32, (reach, BLK), 1) + b * BLK
                valid = (at_j <= at_i) & (at_j < length)
                score = jnp.where(valid, dot_nt(kx[:reach], qx) * factor, -1e30)
                top = jnp.max(score, axis=0, keepdims=True)
                expo = jnp.exp(score - top)
                prob = expo * (1.0 / jnp.sum(expo, axis=0, keepdims=True))
                dprob = dot_nt(vx[:reach], gx)
                delta = jnp.sum(prob * dprob, axis=0, keepdims=True)
                dscore = (prob * (dprob - delta)).astype(BF16)
                dqs[side].append(dot_tn(dscore, kx[:reach]))
                dk_b = dot_nn(dscore, qx)
                dv_b = dot_nn(prob.astype(BF16), gx)
                for j in range(b + 1):
                    part = slice(j * BLK, (j + 1) * BLK)
                    dk[j] = dk_b[part] if dk[j] is None else dk[j] + dk_b[part]
                    dv[j] = dv_b[part] if dv[j] is None else dv[j] + dv_b[part]
            dks.append(jnp.concatenate(dk, axis=0) * factor)
            dvs.append(jnp.concatenate(dv, axis=0))
        for b in range(blocks):
            left, right = dqs[0][b], dqs[1][b]
            dq = jnp.concatenate(
                [left[:, :DN], left[:, DN:] + right[:, :DN], right[:, DN:]], axis=1
            )
            qg[b * BLK : (b + 1) * BLK, qcols] = (dq * factor).astype(BF16)
        rope_acc[:, :DN] += dks[0][:, DN:]
        rope_acc[:, DN:] += dks[1][:, DN:]
        both = jnp.concatenate(
            [
                dks[0][:, :DN].astype(BF16),
                dks[1].astype(BF16)[:, D_R : D_R + DN],
                dvs[0].astype(BF16),
                dvs[1].astype(BF16),
            ],
            axis=1,
        )
        dkv[p] = both
        sums = dot_nn(cont_t[...], both).astype(BF16)
        send[p] = sums.reshape(n_dp, D_C // n_dp, 2 * DN + 2 * DV)
        for o in range(1, n_dp):
            partial(p, o).start()
        return carry

    lax.fori_loop(0, pairs, body, 0)

    lacc[:, :, D_C:] = (
        (rope_acc[:, :D_R] + rope_acc[:, DN + D_R :])
    ).reshape(n_head, tokens, D_R)
    lacc[:, :, :D_C] = jnp.zeros((n_head, tokens, D_C), F32)

    def back(p, carry):
        cols = pl.ds(pl.multiple_of(p * 2 * DN, 2 * DN), 2 * DN)
        term = dot_nt(dkv[p, :, : 2 * DN], wk[:, cols]) + dot_nt(dkv[p, :, 2 * DN :], wv[:, cols])
        lacc[:, :, :D_C] += term.reshape(n_head, tokens, D_C)
        return carry

    lax.fori_loop(0, pairs, back, 0)
    for o in range(1, n_head):
        latent_part(o).start()
    total = lacc[me_h]
    for o in range(1, n_head):
        latent_part(o).wait()
        total = total + lrecv[o - 1]
    lg[...] = total.astype(BF16)

    def finish(p, carry):
        cols = pl.ds(pl.multiple_of(p * 2 * DN, 2 * DN), 2 * DN)
        total = send[p, me_d].astype(F32)
        for o in range(1, n_dp):
            partial(p, o).wait()
            total = total + recv[p, o - 1].astype(F32)
        uk[:, cols] = total[:, : 2 * DN]
        uv[:, cols] = total[:, 2 * DN :]
        return carry

    lax.fori_loop(0, pairs, finish, 0)


def on_device(n_head, n_dp, queries, out_grad, latent, w_uk, w_uv, lengths, rewards, pairing):
    _, length_all, q_width = queries.shape
    tokens = latent.shape[1]
    key_width = w_uk.shape[1]
    pairs = key_width // (2 * DN)
    rows = D_C // n_dp
    vmem = pl.BlockSpec(memory_space=pltpu.VMEM)
    smem = pl.BlockSpec(memory_space=pltpu.SMEM)
    q_grad, latent_grad, uk_grad, uv_grad = pl.pallas_call(
        functools.partial(kernel, n_head, n_dp, pairs),
        out_shape=(
            jax.ShapeDtypeStruct((length_all, q_width), BF16),
            jax.ShapeDtypeStruct((tokens, D_C + D_R), BF16),
            jax.ShapeDtypeStruct((rows, key_width), F32),
            jax.ShapeDtypeStruct((rows, key_width), F32),
        ),
        in_specs=[smem] * 3 + [vmem] * 5,
        out_specs=(vmem,) * 4,
        scratch_shapes=[
            pltpu.VMEM((length_all, D_C + D_R), BF16),
            pltpu.VMEM((D_C, length_all), BF16),
            pltpu.VMEM((pairs, n_dp, rows, 2 * DN + 2 * DV), BF16),
            pltpu.VMEM((pairs, n_dp - 1, rows, 2 * DN + 2 * DV), BF16),
            pltpu.VMEM((pairs, length_all, 2 * DN + 2 * DV), BF16),
            pltpu.VMEM((length_all, 2 * DN), F32),
            pltpu.VMEM((n_head, tokens, D_C + D_R), F32),
            pltpu.VMEM((n_head - 1, tokens, D_C + D_R), F32),
            pltpu.SemaphoreType.DMA((n_head - 1,)),
            pltpu.SemaphoreType.DMA((n_head - 1,)),
            pltpu.SemaphoreType.DMA((pairs, n_dp - 1)),
            pltpu.SemaphoreType.DMA((pairs, n_dp - 1)),
            pltpu.SemaphoreType.DMA((n_head - 1,)),
            pltpu.SemaphoreType.DMA((n_head - 1,)),
        ],
        compiler_params=pltpu.CompilerParams(
            collective_id=0, has_side_effects=True, vmem_limit_bytes=52 * 1024 * 1024
        ),
    )(lengths, rewards, pairing, latent[0], queries[0], out_grad[0], w_uk, w_uv)
    return q_grad[None], latent_grad[None], uk_grad, uv_grad


def solution(mesh):
    in_specs = (
        P(("groups", "dp"), None, "head"),
        P(("groups", "dp"), None, "head"),
        P(("groups", "dp"), "head", None),
        P(None, "head"),
        P(None, "head"),
        P(("groups", "dp")),
        P("groups"),
        P("groups"),
    )
    out_specs = (
        P(("groups", "dp"), None, "head"),
        P(("groups", "dp"), "head", None),
        P(("groups", "dp"), "head"),
        P(("groups", "dp"), "head"),
    )
    return jax.shard_map(
        functools.partial(on_device, mesh.shape["head"], mesh.shape["dp"]),
        mesh=mesh,
        in_specs=in_specs,
        out_specs=out_specs,
        check_vma=False,
    )
```

```python
import functools

import jax
import jax.numpy as jnp
from jax import lax
from jax.experimental import pallas as pl
from jax.experimental.pallas import tpu as pltpu
from jax.sharding import PartitionSpec as P

D_C = 512
D_R = 64
DN = 128
DV = 128
BLK = 256
MESH = pl.DeviceIdType.MESH
F32 = jnp.float32
BF16 = jnp.bfloat16


def dot_nn(a, b):
    return lax.dot_general(a, b, (((1,), (0,)), ((), ())), preferred_element_type=F32)


def dot_nt(a, b):
    return lax.dot_general(a, b, (((1,), (1,)), ((), ())), preferred_element_type=F32)


def dot_tn(a, b):
    return lax.dot_general(a, b, (((0,), (0,)), ((), ())), preferred_element_type=F32)


def own_weight(rewards, pairing, own):
    count = rewards.shape[0]
    diff = jnp.float32(0.0)
    sign = jnp.float32(0.0)
    for k in range(count // 2):
        chosen, rejected = pairing[2 * k], pairing[2 * k + 1]
        gap = jnp.float32(0.0)
        for j in range(count):
            gap = gap + jnp.where(rejected == j, rewards[j], 0.0)
            gap = gap - jnp.where(chosen == j, rewards[j], 0.0)
        diff = jnp.where((chosen == own) | (rejected == own), gap, diff)
        sign = jnp.where(chosen == own, -1.0, jnp.where(rejected == own, 1.0, sign))
    return sign * jax.nn.sigmoid(jnp.full((1, DV), diff, F32))


def kernel(
    n_head, n_dp, pairs,
    lengths, rewards, pairing, latent, q_in, og_in, wk_in, wv_in,
    qg_out, lg, uk, uv,
    q, og, wk, wv, qg, full, cont_t, send, recv, dkv, rope_acc, lacc, lrecv,
    g_send, g_recv, p_send, p_recv, l_send, l_recv, load_sem,
):
    factor = (DN + D_R) ** (-0.5)
    me_h = lax.axis_index("head")
    me_d = lax.axis_index("dp")
    tokens = latent.shape[0]
    length_all = full.shape[0]
    blocks = length_all // BLK
    last = 2
    loads = [
        pltpu.make_async_copy(src, dst, load_sem.at[n])
        for n, (src, dst) in enumerate(((wk_in, wk), (wv_in, wv), (og_in, og), (q_in, q)))
    ]
    for load in loads:
        load.start()

    barrier = pltpu.get_barrier_semaphore()
    for o in range(1, n_head):
        pl.semaphore_signal(
            barrier, inc=1, device_id={"head": lax.rem(me_h + o, n_head)}, device_id_type=MESH
        )
    for o in (1, n_dp - 1):
        pl.semaphore_signal(
            barrier, inc=1, device_id={"dp": lax.rem(me_d + o, n_dp)}, device_id_type=MESH
        )
    pl.semaphore_wait(barrier, n_head + 1)

    own_rows = pl.ds(pl.multiple_of(me_h * tokens, tokens), tokens)

    def gather(o):
        return pltpu.make_async_remote_copy(
            src_ref=latent,
            dst_ref=full.at[own_rows],
            send_sem=g_send.at[o - 1],
            recv_sem=g_recv.at[o - 1],
            device_id={"head": lax.rem(me_h + o, n_head)},
            device_id_type=MESH,
        )

    steps = (lax.rem(me_d + 1, n_dp), lax.rem(me_d + n_dp - 1, n_dp))

    def hop(p, d, way):
        return pltpu.make_async_remote_copy(
            src_ref=send.at[p, d],
            dst_ref=recv.at[p, way, d],
            send_sem=p_send.at[p, d],
            recv_sem=p_recv.at[p, way, d],
            device_id={"dp": steps[way]},
            device_id_type=MESH,
        )

    def forward(p, way):
        order = range(n_dp - 1, 0, -1) if way == 0 else range(n_dp - 1)
        for d in order:

            @pl.when((me_d < d) if way == 0 else (me_d > d))
            def _():
                @pl.when((me_d > 0) if way == 0 else (me_d < n_dp - 1))
                def _():
                    hop(p, d, way).wait_recv()
                    total = send[p, d].astype(F32) + recv[p, way, d].astype(F32)
                    send[p, d] = total.astype(BF16)

                hop(p, d, way).start()

    place = (me_d, n_dp - 1 - me_d)
    lags = tuple(at + (at + n_dp - 1) // n_dp for at in place)

    def latent_part(o):
        peer = lax.rem(me_h + o, n_head)
        return pltpu.make_async_remote_copy(
            src_ref=lacc.at[peer],
            dst_ref=lrecv.at[o - 1],
            send_sem=l_send.at[o - 1],
            recv_sem=l_recv.at[o - 1],
            device_id={"head": peer},
            device_id_type=MESH,
        )

    for o in range(1, n_head):
        gather(o).start()
    full[own_rows, :] = latent[...]
    length = lengths[0]
    weight = own_weight(rewards, pairing, me_d)
    rope_acc[...] = jnp.zeros_like(rope_acc)
    for o in range(1, n_head):
        gather(o).wait()
    cont_t[...] = full[:, :D_C].T
    for load in loads:
        load.wait()

    def body(p, carry):
        cols = pl.ds(pl.multiple_of(p * 2 * DN, 2 * DN), 2 * DN)
        qcols = pl.ds(pl.multiple_of(p * 2 * (DN + D_R), 2 * (DN + D_R)), 2 * (DN + D_R))
        content = full[:, :D_C]
        rope = full[:, D_C:]
        k2 = dot_nn(content, wk[:, cols]).astype(BF16)
        v2 = dot_nn(content, wv[:, cols]).astype(BF16)
        empty = jnp.zeros((length_all, D_R), BF16)
        keys = (
            jnp.concatenate([k2[:, :DN], rope, empty], axis=1),
            jnp.concatenate([empty, k2[:, DN:], rope], axis=1),
        )
        row = lax.broadcasted_iota(jnp.int32, (length_all, 2 * DV), 0)
        w2 = jnp.concatenate([weight, weight], axis=1)
        g2 = og[:, cols].astype(F32) * w2
        g2 = jnp.where(row < length, g2, 0.0).astype(BF16)
        dks, dvs = [], []
        dqs = [[], []]
        for side in range(2):
            kx = keys[side]
            vx = v2[:, side * DV : (side + 1) * DV]
            dk = [None] * blocks
            dv = [None] * blocks
            for b in range(blocks):
                reach = (b + 1) * BLK
                rows = slice(b * BLK, reach)
                qx = q[rows, qcols][:, side * DN : side * DN + 2 * DN]
                gx = g2[rows, side * DV : (side + 1) * DV]
                at_j = lax.broadcasted_iota(jnp.int32, (reach, BLK), 0)
                at_i = lax.broadcasted_iota(jnp.int32, (reach, BLK), 1) + b * BLK
                valid = (at_j <= at_i) & (at_j < length)
                score = jnp.where(valid, dot_nt(kx[:reach], qx) * factor, -1e30)
                top = jnp.max(score, axis=0, keepdims=True)
                expo = jnp.exp(score - top)
                prob = expo * (1.0 / jnp.sum(expo, axis=0, keepdims=True))
                dprob = dot_nt(vx[:reach], gx)
                delta = jnp.sum(prob * dprob, axis=0, keepdims=True)
                dscore = (prob * (dprob - delta)).astype(BF16)
                dqs[side].append(dot_tn(dscore, kx[:reach]))
                dk_b = dot_nn(dscore, qx)
                dv_b = dot_nn(prob.astype(BF16), gx)
                for j in range(b + 1):
                    part = slice(j * BLK, (j + 1) * BLK)
                    dk[j] = dk_b[part] if dk[j] is None else dk[j] + dk_b[part]
                    dv[j] = dv_b[part] if dv[j] is None else dv[j] + dv_b[part]
            dks.append(jnp.concatenate(dk, axis=0) * factor)
            dvs.append(jnp.concatenate(dv, axis=0))
        for b in range(blocks):
            left, right = dqs[0][b], dqs[1][b]
            dq = jnp.concatenate(
                [left[:, :DN], left[:, DN:] + right[:, :DN], right[:, DN:]], axis=1
            )
            qg[b * BLK : (b + 1) * BLK, qcols] = (dq * factor).astype(BF16)
        rope_acc[:, :DN] += dks[0][:, DN:]
        rope_acc[:, DN:] += dks[1][:, DN:]
        both = jnp.concatenate(
            [
                dks[0][:, :DN].astype(BF16),
                dks[1].astype(BF16)[:, D_R : D_R + DN],
                dvs[0].astype(BF16),
                dvs[1].astype(BF16),
            ],
            axis=1,
        )
        dkv[p] = both
        sums = dot_nn(cont_t[...], both).astype(BF16)
        send[p] = sums.reshape(n_dp, D_C // n_dp, 2 * DN + 2 * DV)
        for way in range(2):

            @pl.when(p >= lags[way])
            def _():
                forward(p - lags[way], way)

        return carry

    lax.fori_loop(0, pairs, body, 0)
    store = pltpu.make_async_copy(qg, qg_out, load_sem.at[0])
    store.start()

    lacc[:, :, D_C:] = (
        (rope_acc[:, :D_R] + rope_acc[:, DN + D_R :])
    ).reshape(n_head, tokens, D_R)
    lacc[:, :, :D_C] = jnp.zeros((n_head, tokens, D_C), F32)

    def back(p, carry):
        cols = pl.ds(pl.multiple_of(p * 2 * DN, 2 * DN), 2 * DN)
        term = dot_nt(dkv[p, :, : 2 * DN], wk[:, cols]) + dot_nt(dkv[p, :, 2 * DN :], wv[:, cols])
        lacc[:, :, :D_C] += term.reshape(n_head, tokens, D_C)
        for way in range(2):

            @pl.when((p + lags[way] >= pairs) & (p < pairs - last))
            def _():
                forward(p, way)

        return carry

    lax.fori_loop(0, pairs, back, 0)
    for o in range(1, n_head):
        latent_part(o).start()
    for p in range(pairs - last, pairs):
        for way in range(2):

            @pl.when(p + lags[way] >= pairs)
            def _():
                forward(p, way)

    total = lacc[me_h]
    for o in range(1, n_head):
        latent_part(o).wait()
        total = total + lrecv[o - 1]
    lg[...] = total.astype(BF16)

    def finish(p, carry):
        cols = pl.ds(pl.multiple_of(p * 2 * DN, 2 * DN), 2 * DN)
        total = send[p, me_d].astype(F32)
        uk[:, cols] = total[:, : 2 * DN]
        uv[:, cols] = total[:, 2 * DN :]
        for way in range(2):

            @pl.when(place[way] > 0)
            def _():
                hop(p, me_d, way).wait_recv()
                more = recv[p, way, me_d].astype(F32)
                uk[:, cols] += more[:, : 2 * DN]
                uv[:, cols] += more[:, 2 * DN :]

            for d in range(n_dp):

                @pl.when((me_d < d) if way == 0 else (me_d > d))
                def _():
                    hop(p, d, way).wait_send()

        return carry

    lax.fori_loop(0, pairs, finish, 0)
    store.wait()


def on_device(n_head, n_dp, queries, out_grad, latent, w_uk, w_uv, lengths, rewards, pairing):
    _, length_all, q_width = queries.shape
    tokens = latent.shape[1]
    key_width = w_uk.shape[1]
    pairs = key_width // (2 * DN)
    rows = D_C // n_dp
    vmem = pl.BlockSpec(memory_space=pltpu.VMEM)
    smem = pl.BlockSpec(memory_space=pltpu.SMEM)
    hbm = pl.BlockSpec(memory_space=pl.ANY)
    q_grad, latent_grad, uk_grad, uv_grad = pl.pallas_call(
        functools.partial(kernel, n_head, n_dp, pairs),
        out_shape=(
            jax.ShapeDtypeStruct((length_all, q_width), BF16),
            jax.ShapeDtypeStruct((tokens, D_C + D_R), BF16),
            jax.ShapeDtypeStruct((rows, key_width), F32),
            jax.ShapeDtypeStruct((rows, key_width), F32),
        ),
        in_specs=[smem] * 3 + [vmem] + [hbm] * 4,
        out_specs=(hbm, vmem, vmem, vmem),
        scratch_shapes=[
            pltpu.VMEM((length_all, q_width), BF16),
            pltpu.VMEM((length_all, key_width), BF16),
            pltpu.VMEM((D_C, key_width), BF16),
            pltpu.VMEM((D_C, key_width), BF16),
            pltpu.VMEM((length_all, q_width), BF16),
            pltpu.VMEM((length_all, D_C + D_R), BF16),
            pltpu.VMEM((D_C, length_all), BF16),
            pltpu.VMEM((pairs, n_dp, rows, 2 * DN + 2 * DV), BF16),
            pltpu.VMEM((pairs, 2, n_dp, rows, 2 * DN + 2 * DV), BF16),
            pltpu.VMEM((pairs, length_all, 2 * DN + 2 * DV), BF16),
            pltpu.VMEM((length_all, 2 * DN), F32),
            pltpu.VMEM((n_head, tokens, D_C + D_R), F32),
            pltpu.VMEM((n_head - 1, tokens, D_C + D_R), F32),
            pltpu.SemaphoreType.DMA((n_head - 1,)),
            pltpu.SemaphoreType.DMA((n_head - 1,)),
            pltpu.SemaphoreType.DMA((pairs, n_dp)),
            pltpu.SemaphoreType.DMA((pairs, 2, n_dp)),
            pltpu.SemaphoreType.DMA((n_head - 1,)),
            pltpu.SemaphoreType.DMA((n_head - 1,)),
            pltpu.SemaphoreType.DMA((4,)),
        ],
        compiler_params=pltpu.CompilerParams(
            collective_id=0, has_side_effects=True, vmem_limit_bytes=52 * 1024 * 1024
        ),
    )(lengths, rewards, pairing, latent[0], queries[0], out_grad[0], w_uk, w_uv)
    return q_grad[None], latent_grad[None], uk_grad, uv_grad


def solution(mesh):
    in_specs = (
        P(("groups", "dp"), None, "head"),
        P(("groups", "dp"), None, "head"),
        P(("groups", "dp"), "head", None),
        P(None, "head"),
        P(None, "head"),
        P(("groups", "dp")),
        P("groups"),
        P("groups"),
    )
    out_specs = (
        P(("groups", "dp"), None, "head"),
        P(("groups", "dp"), "head", None),
        P(("groups", "dp"), "head"),
        P(("groups", "dp"), "head"),
    )
    return jax.shard_map(
        functools.partial(on_device, mesh.shape["head"], mesh.shape["dp"]),
        mesh=mesh,
        in_specs=in_specs,
        out_specs=out_specs,
        check_vma=False,
    )
```

```python
import functools

import jax
import jax.numpy as jnp
from jax import lax
from jax.experimental import pallas as pl
from jax.experimental.pallas import tpu as pltpu
from jax.sharding import PartitionSpec as P

D_C = 512
D_R = 64
DN = 128
DV = 128
BLK = 256
MESH = pl.DeviceIdType.MESH
F32 = jnp.float32
BF16 = jnp.bfloat16


def dot_nn(a, b):
    return lax.dot_general(a, b, (((1,), (0,)), ((), ())), preferred_element_type=F32)


def dot_nt(a, b):
    return lax.dot_general(a, b, (((1,), (1,)), ((), ())), preferred_element_type=F32)


def dot_tn(a, b):
    return lax.dot_general(a, b, (((0,), (0,)), ((), ())), preferred_element_type=F32)


def own_weight(rewards, pairing, own):
    count = rewards.shape[0]
    diff = jnp.float32(0.0)
    sign = jnp.float32(0.0)
    for k in range(count // 2):
        chosen, rejected = pairing[2 * k], pairing[2 * k + 1]
        gap = jnp.float32(0.0)
        for j in range(count):
            gap = gap + jnp.where(rejected == j, rewards[j], 0.0)
            gap = gap - jnp.where(chosen == j, rewards[j], 0.0)
        diff = jnp.where((chosen == own) | (rejected == own), gap, diff)
        sign = jnp.where(chosen == own, -1.0, jnp.where(rejected == own, 1.0, sign))
    return sign * jax.nn.sigmoid(jnp.full((1, DV), diff, F32))


def kernel(
    n_head, n_dp, pairs,
    lengths, rewards, pairing, latent, q_in, og_in, wk_in, wv_in,
    qg_out, lg, uk, uv,
    q, og, wk, wv, qg, full, cont_t, send, recv, dkv, rope_acc, lacc, lsend, lrecv,
    g_send, g_recv, p_send, p_recv, l_send, l_recv, load_sem,
):
    factor = (DN + D_R) ** (-0.5)
    me_h = lax.axis_index("head")
    me_d = lax.axis_index("dp")
    tokens = latent.shape[0]
    length_all = full.shape[0]
    blocks = length_all // BLK
    last = 2
    loads = [
        pltpu.make_async_copy(src, dst, load_sem.at[n])
        for n, (src, dst) in enumerate(((wk_in, wk), (wv_in, wv), (og_in, og), (q_in, q)))
    ]
    for load in loads:
        load.start()

    barrier = pltpu.get_barrier_semaphore()
    for o in range(1, n_head):
        pl.semaphore_signal(
            barrier, inc=1, device_id={"head": lax.rem(me_h + o, n_head)}, device_id_type=MESH
        )
    for o in (1, n_dp - 1):
        pl.semaphore_signal(
            barrier, inc=1, device_id={"dp": lax.rem(me_d + o, n_dp)}, device_id_type=MESH
        )
    pl.semaphore_wait(barrier, n_head + 1)

    own_rows = pl.ds(pl.multiple_of(me_h * tokens, tokens), tokens)

    def gather(o):
        return pltpu.make_async_remote_copy(
            src_ref=latent,
            dst_ref=full.at[own_rows],
            send_sem=g_send.at[o - 1],
            recv_sem=g_recv.at[o - 1],
            device_id={"head": lax.rem(me_h + o, n_head)},
            device_id_type=MESH,
        )

    steps = (lax.rem(me_d + 1, n_dp), lax.rem(me_d + n_dp - 1, n_dp))

    def hop(p, d, way):
        return pltpu.make_async_remote_copy(
            src_ref=send.at[p, d],
            dst_ref=recv.at[p, way, d],
            send_sem=p_send.at[p, d],
            recv_sem=p_recv.at[p, way, d],
            device_id={"dp": steps[way]},
            device_id_type=MESH,
        )

    def forward(p, way):
        order = range(n_dp - 1, 0, -1) if way == 0 else range(n_dp - 1)
        for d in order:

            @pl.when((me_d < d) if way == 0 else (me_d > d))
            def _():
                @pl.when((me_d > 0) if way == 0 else (me_d < n_dp - 1))
                def _():
                    hop(p, d, way).wait_recv()
                    total = send[p, d].astype(F32) + recv[p, way, d].astype(F32)
                    send[p, d] = total.astype(BF16)

                hop(p, d, way).start()

    place = (me_d, n_dp - 1 - me_d)
    lags = tuple(at + 0 for at in place)

    def latent_part(o):
        peer = lax.rem(me_h + o, n_head)
        return pltpu.make_async_remote_copy(
            src_ref=lsend.at[peer],
            dst_ref=lrecv.at[o - 1],
            send_sem=l_send.at[o - 1],
            recv_sem=l_recv.at[o - 1],
            device_id={"head": peer},
            device_id_type=MESH,
        )

    for o in range(1, n_head):
        gather(o).start()
    full[own_rows, :] = latent[...]
    length = lengths[0]
    weight = own_weight(rewards, pairing, me_d)
    rope_acc[...] = jnp.zeros_like(rope_acc)
    for o in range(1, n_head):
        gather(o).wait()
    cont_t[...] = full[:, :D_C].T
    for load in loads:
        load.wait()

    def body(p, carry):
        cols = pl.ds(pl.multiple_of(p * 2 * DN, 2 * DN), 2 * DN)
        qcols = pl.ds(pl.multiple_of(p * 2 * (DN + D_R), 2 * (DN + D_R)), 2 * (DN + D_R))
        content = full[:, :D_C]
        rope = full[:, D_C:]
        k2 = dot_nn(content, wk[:, cols]).astype(BF16)
        v2 = dot_nn(content, wv[:, cols]).astype(BF16)
        empty = jnp.zeros((length_all, D_R), BF16)
        keys = (
            jnp.concatenate([k2[:, :DN], rope, empty], axis=1),
            jnp.concatenate([empty, k2[:, DN:], rope], axis=1),
        )
        row = lax.broadcasted_iota(jnp.int32, (length_all, 2 * DV), 0)
        w2 = jnp.concatenate([weight, weight], axis=1)
        g2 = og[:, cols].astype(F32) * w2
        g2 = jnp.where(row < length, g2, 0.0).astype(BF16)
        dks, dvs = [], []
        dqs = [[], []]
        for side in range(2):
            kx = keys[side]
            vx = v2[:, side * DV : (side + 1) * DV]
            dk = [None] * blocks
            dv = [None] * blocks
            for b in range(blocks):
                reach = (b + 1) * BLK
                rows = slice(b * BLK, reach)
                qx = q[rows, qcols][:, side * DN : side * DN + 2 * DN]
                gx = g2[rows, side * DV : (side + 1) * DV]
                at_j = lax.broadcasted_iota(jnp.int32, (reach, BLK), 0)
                at_i = lax.broadcasted_iota(jnp.int32, (reach, BLK), 1) + b * BLK
                valid = (at_j <= at_i) & (at_j < length)
                score = jnp.where(valid, dot_nt(kx[:reach], qx) * factor, -1e30)
                top = jnp.max(score, axis=0, keepdims=True)
                expo = jnp.exp(score - top)
                prob = expo * (1.0 / jnp.sum(expo, axis=0, keepdims=True))
                dprob = dot_nt(vx[:reach], gx)
                delta = jnp.sum(prob * dprob, axis=0, keepdims=True)
                dscore = (prob * (dprob - delta)).astype(BF16)
                dqs[side].append(dot_tn(dscore, kx[:reach]))
                dk_b = dot_nn(dscore, qx)
                dv_b = dot_nn(prob.astype(BF16), gx)
                for j in range(b + 1):
                    part = slice(j * BLK, (j + 1) * BLK)
                    dk[j] = dk_b[part] if dk[j] is None else dk[j] + dk_b[part]
                    dv[j] = dv_b[part] if dv[j] is None else dv[j] + dv_b[part]
            dks.append(jnp.concatenate(dk, axis=0) * factor)
            dvs.append(jnp.concatenate(dv, axis=0))
        for b in range(blocks):
            left, right = dqs[0][b], dqs[1][b]
            dq = jnp.concatenate(
                [left[:, :DN], left[:, DN:] + right[:, :DN], right[:, DN:]], axis=1
            )
            qg[b * BLK : (b + 1) * BLK, qcols] = (dq * factor).astype(BF16)
        rope_acc[:, :DN] += dks[0][:, DN:]
        rope_acc[:, DN:] += dks[1][:, DN:]
        both = jnp.concatenate(
            [
                dks[0][:, :DN].astype(BF16),
                dks[1].astype(BF16)[:, D_R : D_R + DN],
                dvs[0].astype(BF16),
                dvs[1].astype(BF16),
            ],
            axis=1,
        )
        dkv[p] = both
        sums = dot_nn(cont_t[...], both).astype(BF16)
        send[p] = sums.reshape(n_dp, D_C // n_dp, 2 * DN + 2 * DV)
        for way in range(2):

            @pl.when(p >= lags[way])
            def _():
                forward(p - lags[way], way)

        return carry

    lax.fori_loop(0, pairs, body, 0)
    store = pltpu.make_async_copy(qg, qg_out, load_sem.at[0])
    store.start()

    lacc[:, :, D_C:] = (
        (rope_acc[:, :D_R] + rope_acc[:, DN + D_R :])
    ).reshape(n_head, tokens, D_R)
    lacc[:, :, :D_C] = jnp.zeros((n_head, tokens, D_C), F32)

    def back(p, carry):
        cols = pl.ds(pl.multiple_of(p * 2 * DN, 2 * DN), 2 * DN)
        term = dot_nt(dkv[p, :, : 2 * DN], wk[:, cols]) + dot_nt(dkv[p, :, 2 * DN :], wv[:, cols])
        lacc[:, :, :D_C] += term.reshape(n_head, tokens, D_C)
        for way in range(2):

            @pl.when((p + lags[way] >= pairs) & (p < pairs - last))
            def _():
                forward(p, way)

        return carry

    lax.fori_loop(0, pairs, back, 0)
    lsend[...] = lacc[...].astype(BF16)
    for o in range(1, n_head):
        latent_part(o).start()
    for p in range(pairs - last, pairs):
        for way in range(2):

            @pl.when(p + lags[way] >= pairs)
            def _():
                forward(p, way)

    total = lacc[me_h]
    for o in range(1, n_head):
        latent_part(o).wait()
        total = total + lrecv[o - 1].astype(F32)
    lg[...] = total.astype(BF16)

    def finish(p, carry):
        cols = pl.ds(pl.multiple_of(p * 2 * DN, 2 * DN), 2 * DN)
        total = send[p, me_d].astype(F32)
        uk[:, cols] = total[:, : 2 * DN]
        uv[:, cols] = total[:, 2 * DN :]
        for way in range(2):

            @pl.when(place[way] > 0)
            def _():
                hop(p, me_d, way).wait_recv()
                more = recv[p, way, me_d].astype(F32)
                uk[:, cols] += more[:, : 2 * DN]
                uv[:, cols] += more[:, 2 * DN :]

            for d in range(n_dp):

                @pl.when((me_d < d) if way == 0 else (me_d > d))
                def _():
                    hop(p, d, way).wait_send()

        return carry

    lax.fori_loop(0, pairs, finish, 0)
    store.wait()


def on_device(n_head, n_dp, queries, out_grad, latent, w_uk, w_uv, lengths, rewards, pairing):
    _, length_all, q_width = queries.shape
    tokens = latent.shape[1]
    key_width = w_uk.shape[1]
    pairs = key_width // (2 * DN)
    rows = D_C // n_dp
    vmem = pl.BlockSpec(memory_space=pltpu.VMEM)
    smem = pl.BlockSpec(memory_space=pltpu.SMEM)
    hbm = pl.BlockSpec(memory_space=pl.ANY)
    q_grad, latent_grad, uk_grad, uv_grad = pl.pallas_call(
        functools.partial(kernel, n_head, n_dp, pairs),
        out_shape=(
            jax.ShapeDtypeStruct((length_all, q_width), BF16),
            jax.ShapeDtypeStruct((tokens, D_C + D_R), BF16),
            jax.ShapeDtypeStruct((rows, key_width), F32),
            jax.ShapeDtypeStruct((rows, key_width), F32),
        ),
        in_specs=[smem] * 3 + [vmem] + [hbm] * 4,
        out_specs=(hbm, vmem, vmem, vmem),
        scratch_shapes=[
            pltpu.VMEM((length_all, q_width), BF16),
            pltpu.VMEM((length_all, key_width), BF16),
            pltpu.VMEM((D_C, key_width), BF16),
            pltpu.VMEM((D_C, key_width), BF16),
            pltpu.VMEM((length_all, q_width), BF16),
            pltpu.VMEM((length_all, D_C + D_R), BF16),
            pltpu.VMEM((D_C, length_all), BF16),
            pltpu.VMEM((pairs, n_dp, rows, 2 * DN + 2 * DV), BF16),
            pltpu.VMEM((pairs, 2, n_dp, rows, 2 * DN + 2 * DV), BF16),
            pltpu.VMEM((pairs, length_all, 2 * DN + 2 * DV), BF16),
            pltpu.VMEM((length_all, 2 * DN), F32),
            pltpu.VMEM((n_head, tokens, D_C + D_R), F32),
            pltpu.VMEM((n_head, tokens, D_C + D_R), BF16),
            pltpu.VMEM((n_head - 1, tokens, D_C + D_R), BF16),
            pltpu.SemaphoreType.DMA((n_head - 1,)),
            pltpu.SemaphoreType.DMA((n_head - 1,)),
            pltpu.SemaphoreType.DMA((pairs, n_dp)),
            pltpu.SemaphoreType.DMA((pairs, 2, n_dp)),
            pltpu.SemaphoreType.DMA((n_head - 1,)),
            pltpu.SemaphoreType.DMA((n_head - 1,)),
            pltpu.SemaphoreType.DMA((4,)),
        ],
        compiler_params=pltpu.CompilerParams(
            collective_id=0, has_side_effects=True, vmem_limit_bytes=52 * 1024 * 1024
        ),
    )(lengths, rewards, pairing, latent[0], queries[0], out_grad[0], w_uk, w_uv)
    return q_grad[None], latent_grad[None], uk_grad, uv_grad


def solution(mesh):
    in_specs = (
        P(("groups", "dp"), None, "head"),
        P(("groups", "dp"), None, "head"),
        P(("groups", "dp"), "head", None),
        P(None, "head"),
        P(None, "head"),
        P(("groups", "dp")),
        P("groups"),
        P("groups"),
    )
    out_specs = (
        P(("groups", "dp"), None, "head"),
        P(("groups", "dp"), "head", None),
        P(("groups", "dp"), "head"),
        P(("groups", "dp"), "head"),
    )
    return jax.shard_map(
        functools.partial(on_device, mesh.shape["head"], mesh.shape["dp"]),
        mesh=mesh,
        in_specs=in_specs,
        out_specs=out_specs,
        check_vma=False,
    )
```

```python
import functools

import jax
import jax.numpy as jnp
from jax import lax
from jax.experimental import pallas as pl
from jax.experimental.pallas import tpu as pltpu
from jax.sharding import PartitionSpec as P

D_C = 512
D_R = 64
DN = 128
DV = 128
BLK = 256
MESH = pl.DeviceIdType.MESH
F32 = jnp.float32
BF16 = jnp.bfloat16


def dot_nn(a, b):
    return lax.dot_general(a, b, (((1,), (0,)), ((), ())), preferred_element_type=F32)


def dot_nt(a, b):
    return lax.dot_general(a, b, (((1,), (1,)), ((), ())), preferred_element_type=F32)


def dot_tn(a, b):
    return lax.dot_general(a, b, (((0,), (0,)), ((), ())), preferred_element_type=F32)


def own_weight(rewards, pairing, own):
    count = rewards.shape[0]
    diff = jnp.float32(0.0)
    sign = jnp.float32(0.0)
    for k in range(count // 2):
        chosen, rejected = pairing[2 * k], pairing[2 * k + 1]
        gap = jnp.float32(0.0)
        for j in range(count):
            gap = gap + jnp.where(rejected == j, rewards[j], 0.0)
            gap = gap - jnp.where(chosen == j, rewards[j], 0.0)
        diff = jnp.where((chosen == own) | (rejected == own), gap, diff)
        sign = jnp.where(chosen == own, -1.0, jnp.where(rejected == own, 1.0, sign))
    return sign * jax.nn.sigmoid(jnp.full((1, DV), diff, F32))


def kernel(
    n_head, n_dp, pairs,
    lengths, rewards, pairing, latent, q_in, og_in, wk_in, wv_in,
    qg_out, lg, uk, uv,
    q, og, wk, wv, qg, full, cont_t, send, recv, dkv, rope_acc, lacc, lsend, lrecv,
    g_send, g_recv, p_send, p_recv, l_send, l_recv, load_sem,
):
    factor = (DN + D_R) ** (-0.5)
    me_h = lax.axis_index("head")
    me_d = lax.axis_index("dp")
    tokens = latent.shape[0]
    length_all = full.shape[0]
    blocks = length_all // BLK
    last = 2
    loads = [
        pltpu.make_async_copy(src, dst, load_sem.at[n])
        for n, (src, dst) in enumerate(((wk_in, wk), (wv_in, wv), (og_in, og), (q_in, q)))
    ]
    for load in loads:
        load.start()

    barrier = pltpu.get_barrier_semaphore()
    for o in range(1, n_head):
        pl.semaphore_signal(
            barrier, inc=1, device_id={"head": lax.rem(me_h + o, n_head)}, device_id_type=MESH
        )
    for o in (1, n_dp - 1):
        pl.semaphore_signal(
            barrier, inc=1, device_id={"dp": lax.rem(me_d + o, n_dp)}, device_id_type=MESH
        )
    pl.semaphore_wait(barrier, n_head + 1)

    own_rows = pl.ds(pl.multiple_of(me_h * tokens, tokens), tokens)

    def gather(o):
        return pltpu.make_async_remote_copy(
            src_ref=latent,
            dst_ref=full.at[own_rows],
            send_sem=g_send.at[o - 1],
            recv_sem=g_recv.at[o - 1],
            device_id={"head": lax.rem(me_h + o, n_head)},
            device_id_type=MESH,
        )

    steps = (lax.rem(me_d + 1, n_dp), lax.rem(me_d + n_dp - 1, n_dp))

    def hop(p, d, way):
        return pltpu.make_async_remote_copy(
            src_ref=send.at[p, d],
            dst_ref=recv.at[p, way, d],
            send_sem=p_send.at[p, d],
            recv_sem=p_recv.at[p, way, d],
            device_id={"dp": steps[way]},
            device_id_type=MESH,
        )

    def forward(p, way):
        order = range(n_dp - 1, 0, -1) if way == 0 else range(n_dp - 1)
        for d in order:

            @pl.when((me_d < d) if way == 0 else (me_d > d))
            def _():
                @pl.when((me_d > 0) if way == 0 else (me_d < n_dp - 1))
                def _():
                    hop(p, d, way).wait_recv()
                    total = send[p, d].astype(F32) + recv[p, way, d].astype(F32)
                    send[p, d] = total.astype(BF16)

                hop(p, d, way).start()

    place = (me_d, n_dp - 1 - me_d)
    lags = tuple(at + 0 for at in place)

    def latent_part(o):
        peer = lax.rem(me_h + o, n_head)
        return pltpu.make_async_remote_copy(
            src_ref=lsend.at[peer],
            dst_ref=lrecv.at[o - 1],
            send_sem=l_send.at[o - 1],
            recv_sem=l_recv.at[o - 1],
            device_id={"head": peer},
            device_id_type=MESH,
        )

    for o in range(1, n_head):
        gather(o).start()
    full[own_rows, :] = latent[...]
    length = lengths[0]
    weight = own_weight(rewards, pairing, me_d)
    rope_acc[...] = jnp.zeros_like(rope_acc)
    for o in range(1, n_head):
        gather(o).wait()
    cont_t[...] = full[:, :D_C].T
    for load in loads:
        load.wait()

    def body(p, carry):
        cols = pl.ds(pl.multiple_of(p * 2 * DN, 2 * DN), 2 * DN)
        qcols = pl.ds(pl.multiple_of(p * 2 * (DN + D_R), 2 * (DN + D_R)), 2 * (DN + D_R))
        content = full[:, :D_C]
        rope = full[:, D_C:]
        k2 = dot_nn(content, wk[:, cols]).astype(BF16)
        v2 = dot_nn(content, wv[:, cols]).astype(BF16)
        empty = jnp.zeros((length_all, D_R), BF16)
        keys = (
            jnp.concatenate([k2[:, :DN], rope, empty], axis=1),
            jnp.concatenate([empty, k2[:, DN:], rope], axis=1),
        )
        row = lax.broadcasted_iota(jnp.int32, (length_all, 2 * DV), 0)
        w2 = jnp.concatenate([weight, weight], axis=1)
        g2 = og[:, cols].astype(F32) * w2
        g2 = jnp.where(row < length, g2, 0.0).astype(BF16)
        dks, dvs = [], []
        dqs = [[], []]
        for side in range(2):
            kx = keys[side]
            vx = v2[:, side * DV : (side + 1) * DV]
            dk = [None] * blocks
            dv = [None] * blocks
            for b in range(blocks):
                reach = (b + 1) * BLK
                rows = slice(b * BLK, reach)
                qx = q[rows, qcols][:, side * DN : side * DN + 2 * DN]
                gx = g2[rows, side * DV : (side + 1) * DV]
                at_j = lax.broadcasted_iota(jnp.int32, (reach, BLK), 0)
                at_i = lax.broadcasted_iota(jnp.int32, (reach, BLK), 1) + b * BLK
                valid = (at_j <= at_i) & (at_j < length)
                score = jnp.where(valid, dot_nt(kx[:reach], qx) * factor, -1e30)
                top = jnp.max(score, axis=0, keepdims=True)
                expo = jnp.exp(score - top)
                prob = expo * (1.0 / jnp.sum(expo, axis=0, keepdims=True))
                dprob = dot_nt(vx[:reach], gx)
                delta = jnp.sum(prob * dprob, axis=0, keepdims=True)
                dscore = (prob * (dprob - delta)).astype(BF16)
                dqs[side].append(dot_tn(dscore, kx[:reach]))
                dk_b = dot_nn(dscore, qx)
                dv_b = dot_nn(prob.astype(BF16), gx)
                for j in range(b + 1):
                    part = slice(j * BLK, (j + 1) * BLK)
                    dk[j] = dk_b[part] if dk[j] is None else dk[j] + dk_b[part]
                    dv[j] = dv_b[part] if dv[j] is None else dv[j] + dv_b[part]
            dks.append(jnp.concatenate(dk, axis=0) * factor)
            dvs.append(jnp.concatenate(dv, axis=0))
        for b in range(blocks):
            left, right = dqs[0][b], dqs[1][b]
            dq = jnp.concatenate(
                [left[:, :DN], left[:, DN:] + right[:, :DN], right[:, DN:]], axis=1
            )
            qg[b * BLK : (b + 1) * BLK, qcols] = (dq * factor).astype(BF16)
        rope_acc[:, :DN] += dks[0][:, DN:]
        rope_acc[:, DN:] += dks[1][:, DN:]
        both = jnp.concatenate(
            [
                dks[0][:, :DN].astype(BF16),
                dks[1].astype(BF16)[:, D_R : D_R + DN],
                dvs[0].astype(BF16),
                dvs[1].astype(BF16),
            ],
            axis=1,
        )
        dkv[p] = both
        sums = dot_nn(cont_t[...], both).astype(BF16)
        send[p] = sums.reshape(n_dp, D_C // n_dp, 2 * DN + 2 * DV)
        for way in range(2):

            @pl.when(p >= lags[way])
            def _():
                forward(p - lags[way], way)

        return carry

    lax.fori_loop(0, pairs, body, 0)
    store = pltpu.make_async_copy(qg, qg_out, load_sem.at[0])
    store.start()

    lacc[:, :, D_C:] = (
        (rope_acc[:, :D_R] + rope_acc[:, DN + D_R :])
    ).reshape(n_head, tokens, D_R)
    lacc[:, :, :D_C] = jnp.zeros((n_head, tokens, D_C), F32)

    def back(p, carry):
        cols = pl.ds(pl.multiple_of(p * 2 * DN, 2 * DN), 2 * DN)
        term = dot_nt(dkv[p, :, : 2 * DN], wk[:, cols]) + dot_nt(dkv[p, :, 2 * DN :], wv[:, cols])
        lacc[:, :, :D_C] += term.reshape(n_head, tokens, D_C)
        for way in range(2):

            @pl.when((p + lags[way] >= pairs) & (p < pairs - last))
            def _():
                forward(p, way)

        return carry

    lax.fori_loop(0, pairs, back, 0)
    lsend[...] = lacc[...].astype(BF16)
    for o in range(1, n_head):
        latent_part(o).start()
    def finish(p, carry):
        cols = pl.ds(pl.multiple_of(p * 2 * DN, 2 * DN), 2 * DN)
        total = send[p, me_d].astype(F32)
        uk[:, cols] = total[:, : 2 * DN]
        uv[:, cols] = total[:, 2 * DN :]
        for way in range(2):

            @pl.when(place[way] > 0)
            def _():
                hop(p, me_d, way).wait_recv()
                more = recv[p, way, me_d].astype(F32)
                uk[:, cols] += more[:, : 2 * DN]
                uv[:, cols] += more[:, 2 * DN :]

            for d in range(n_dp):

                @pl.when((me_d < d) if way == 0 else (me_d > d))
                def _():
                    hop(p, d, way).wait_send()

        return carry

    for p in range(pairs - last, pairs):
        if p == pairs - 1:
            lax.fori_loop(0, pairs - last, finish, 0)
        for way in range(2):

            @pl.when(p + lags[way] >= pairs)
            def _():
                forward(p, way)

    total = lacc[me_h]
    for o in range(1, n_head):
        latent_part(o).wait()
        total = total + lrecv[o - 1].astype(F32)
    lg[...] = total.astype(BF16)

    lax.fori_loop(pairs - last, pairs, finish, 0)
    store.wait()


def on_device(n_head, n_dp, queries, out_grad, latent, w_uk, w_uv, lengths, rewards, pairing):
    _, length_all, q_width = queries.shape
    tokens = latent.shape[1]
    key_width = w_uk.shape[1]
    pairs = key_width // (2 * DN)
    rows = D_C // n_dp
    vmem = pl.BlockSpec(memory_space=pltpu.VMEM)
    smem = pl.BlockSpec(memory_space=pltpu.SMEM)
    hbm = pl.BlockSpec(memory_space=pl.ANY)
    q_grad, latent_grad, uk_grad, uv_grad = pl.pallas_call(
        functools.partial(kernel, n_head, n_dp, pairs),
        out_shape=(
            jax.ShapeDtypeStruct((length_all, q_width), BF16),
            jax.ShapeDtypeStruct((tokens, D_C + D_R), BF16),
            jax.ShapeDtypeStruct((rows, key_width), F32),
            jax.ShapeDtypeStruct((rows, key_width), F32),
        ),
        in_specs=[smem] * 3 + [vmem] + [hbm] * 4,
        out_specs=(hbm, vmem, vmem, vmem),
        scratch_shapes=[
            pltpu.VMEM((length_all, q_width), BF16),
            pltpu.VMEM((length_all, key_width), BF16),
            pltpu.VMEM((D_C, key_width), BF16),
            pltpu.VMEM((D_C, key_width), BF16),
            pltpu.VMEM((length_all, q_width), BF16),
            pltpu.VMEM((length_all, D_C + D_R), BF16),
            pltpu.VMEM((D_C, length_all), BF16),
            pltpu.VMEM((pairs, n_dp, rows, 2 * DN + 2 * DV), BF16),
            pltpu.VMEM((pairs, 2, n_dp, rows, 2 * DN + 2 * DV), BF16),
            pltpu.VMEM((pairs, length_all, 2 * DN + 2 * DV), BF16),
            pltpu.VMEM((length_all, 2 * DN), F32),
            pltpu.VMEM((n_head, tokens, D_C + D_R), F32),
            pltpu.VMEM((n_head, tokens, D_C + D_R), BF16),
            pltpu.VMEM((n_head - 1, tokens, D_C + D_R), BF16),
            pltpu.SemaphoreType.DMA((n_head - 1,)),
            pltpu.SemaphoreType.DMA((n_head - 1,)),
            pltpu.SemaphoreType.DMA((pairs, n_dp)),
            pltpu.SemaphoreType.DMA((pairs, 2, n_dp)),
            pltpu.SemaphoreType.DMA((n_head - 1,)),
            pltpu.SemaphoreType.DMA((n_head - 1,)),
            pltpu.SemaphoreType.DMA((4,)),
        ],
        compiler_params=pltpu.CompilerParams(
            collective_id=0, has_side_effects=True, vmem_limit_bytes=52 * 1024 * 1024
        ),
    )(lengths, rewards, pairing, latent[0], queries[0], out_grad[0], w_uk, w_uv)
    return q_grad[None], latent_grad[None], uk_grad, uv_grad


def solution(mesh):
    in_specs = (
        P(("groups", "dp"), None, "head"),
        P(("groups", "dp"), None, "head"),
        P(("groups", "dp"), "head", None),
        P(None, "head"),
        P(None, "head"),
        P(("groups", "dp")),
        P("groups"),
        P("groups"),
    )
    out_specs = (
        P(("groups", "dp"), None, "head"),
        P(("groups", "dp"), "head", None),
        P(("groups", "dp"), "head"),
        P(("groups", "dp"), "head"),
    )
    return jax.shard_map(
        functools.partial(on_device, mesh.shape["head"], mesh.shape["dp"]),
        mesh=mesh,
        in_specs=in_specs,
        out_specs=out_specs,
        check_vma=False,
    )
```
